512 devices in a mesh: snap: 16 (over x, y), vert: 32 (over z, core).
Axes of the slice: x: 4, y: 4, z: 16, core: 2. Of those that a mesh axis runs over, the one named last changes fastest.
Arguments:
- features: bfloat16 [16, 16384, 256], P('snap', 'vert'), may hold values from -6 to 6
- tile_src: int32 [16, 1024], P('snap', 'vert'), may hold values from 0 to 127, as said below
- tile_dst: int32 [16, 1024], P('snap', 'vert'), may hold values from 0 to 127, as said below
- tile_count: int32 [16, 32], P('snap', 'vert'), may hold values from 4 to 32, as said below
- tile_vals: bfloat16 [16, 1024, 128, 128], P('snap', 'vert'), may hold values from -0.25 to 0.25
- norm_gain: float32 [256], replicated, may hold values from 0.25 to 1.75
- mix_weight: bfloat16 [256, 512], replicated, may hold values from -0.375 to 0.375
- decay_rate: float32 [16, 256], replicated, may hold values from 0 to 9, as said below
- mlp_gain: float32 [256], replicated, may hold values from 0.25 to 1.75
- up_weight: bfloat16 [256, 1024], replicated, may hold values from -0.375 to 0.375
- down_weight: bfloat16 [1024, 256], replicated, may hold values from -0.1875 to 0.1875
- link_weight: bfloat16 [256, 256], replicated, may hold values from -0.375 to 0.375
- pair_left: int32 [16, 1024], P('snap', 'vert'), may hold values from 0 to 127, as said below
- pair_right: int32 [16, 1024], P('snap', 'vert'), may hold values from 0 to 127, as said below
Outputs:
- embeddings: bfloat16 [16, 16384, 256], P('snap', 'vert')
- scores: bfloat16 [16, 1024, 128, 128], P('snap', 'vert')
The draws below stay inside these ranges and needn't reach their ends.
Inputs may be any that keep to these rules, and one draw needn't show every extreme that they name: `tile_src`: a slot of vertex part p names a source block from p * 4 - 4 to p * 4 + 2 * 4 - 1. `tile_dst`: a slot of vertex part p names a destination block of that part, p * 4 to p * 4 + 3. `tile_count`: in every snapshot some vertex part has all 32 slots live. `decay_rate`: decay rates are positive. `pair_left`: a pair of vertex part p has its first block in that part, p * 4 to p * 4 + 3. `pair_right`: a pair of vertex part p has its second block from p * 4 - 4 to p * 4 + 2 * 4 - 1.
All inputs are finite; a program needn't handle non-finite values.
Results may differ from the reference program's by a relative error of at most 0.0091.
Values may be sent and summed in bfloat16 or wider, within the bound.
No kernel may reach another device: no remote copies, remote signals or barrier semaphores. Data moves between devices by JAX's collectives and lax.ppermute only.
A program may use at most 64 MiB of HBM per device.

```python
import math
import jax
import jax.numpy as jnp
from jax import lax

F = 256
HID = 1024
TILE = 128
TILE_CAP = 32
PAIRS_DEV = 32
SNAPSHOT_COUNT = 16
V = 16384
NB = 128
BPD = 4
N_VERT = 32


def source_blocks(subkey, per_part):
    owners = jnp.arange(N_VERT * per_part, dtype=jnp.int32) // per_part
    offsets = jax.random.randint(subkey, (SNAPSHOT_COUNT, N_VERT * per_part), 0, 3 * BPD, dtype=jnp.int32)
    blocks = owners[None, :] * BPD - BPD + offsets
    blocks = jnp.where(blocks < 0, blocks + BPD, blocks)
    blocks = jnp.where(blocks >= NB, blocks - BPD, blocks)
    return blocks.astype(jnp.int32)


def owned_blocks(subkey, per_part):
    owners = jnp.arange(N_VERT * per_part, dtype=jnp.int32) // per_part
    offsets = jax.random.randint(subkey, (SNAPSHOT_COUNT, N_VERT * per_part), 0, BPD, dtype=jnp.int32)
    return (owners[None, :] * BPD + offsets).astype(jnp.int32)


def draw_tile_src(key, part):
    return source_blocks(jax.random.fold_in(key, 11), TILE_CAP)


def draw_tile_dst(key, part):
    return owned_blocks(jax.random.fold_in(key, 12), TILE_CAP)


def draw_tile_count(key, part):
    counts = jax.random.randint(jax.random.fold_in(key, 13), (SNAPSHOT_COUNT, N_VERT), TILE_CAP // 8, TILE_CAP // 2 + 1, dtype=jnp.int32)
    fullest = jax.random.randint(jax.random.fold_in(key, 14), (SNAPSHOT_COUNT, 1), 0, N_VERT, dtype=jnp.int32)
    column_ids = jnp.arange(N_VERT, dtype=jnp.int32)[None, :]
    return jnp.where(column_ids == fullest, TILE_CAP, counts).astype(jnp.int32)


def draw_pair_left(key, part):
    return owned_blocks(jax.random.fold_in(key, 21), PAIRS_DEV)


def draw_pair_right(key, part):
    return source_blocks(jax.random.fold_in(key, 23), PAIRS_DEV)


def draw_decay_rate(key, part):
    child_keys = jax.random.split(jax.random.fold_in(key, 17), 5)
    slow_share = 0.5
    slow_mask = jax.random.uniform(child_keys[0], (F,), dtype=jnp.float32) < slow_share
    slow_rates = jnp.exp(jax.random.uniform(child_keys[1], (F,), dtype=jnp.float32, minval=math.log(0.16 / SNAPSHOT_COUNT), maxval=math.log(2.2 / SNAPSHOT_COUNT)))
    fast_rates = jnp.exp(jax.random.uniform(child_keys[2], (F,), dtype=jnp.float32, minval=0.0, maxval=math.log(4.0)))
    rate_dispersion = jnp.exp(jax.random.uniform(child_keys[3], (SNAPSHOT_COUNT, F), dtype=jnp.float32, minval=math.log(0.5), maxval=math.log(2.0)))
    spike_events = jax.random.randint(child_keys[4], (3,), 0, SNAPSHOT_COUNT, dtype=jnp.int32)
    spike_rows = jnp.any(jnp.arange(SNAPSHOT_COUNT, dtype=jnp.int32)[:, None] == spike_events[None, :], axis=1)
    baseline_rates = jnp.where(slow_mask, slow_rates, fast_rates)
    arrival_rates = baseline_rates[None, :] * rate_dispersion + jnp.where(spike_rows, 1.0, 0.0)[:, None]
    return arrival_rates.astype(jnp.float32)


def levels(key, extent, shards, least, largest):
    factor_of = 1.0
    for axis_at, shards_of in shards:
        steps = jax.random.uniform(jax.random.fold_in(jax.random.fold_in(key, 6), axis_at), (shards_of,), jnp.float32, least / len(shards), largest / len(shards))
        factor_of = factor_of * jnp.repeat(jnp.exp(steps), extent[axis_at] // shards_of).reshape((-1,) + (1,) * (len(extent) - 1 - axis_at))
    return factor_of


def gaussian(stream_key, shape, scale, limit, cuts=(), kind=jnp.bfloat16):
    values = scale * jax.random.normal(stream_key, shape, jnp.float32)
    if cuts:
        values = values * levels(stream_key, shape, cuts, -0.22, 0.18)
    return jnp.clip(values, -limit, limit).astype(kind)


def setup_inputs(seed: int = 0) -> dict:
    arg_keys = jax.random.split(jax.random.key(seed), 15)
    return {
        "features": gaussian(arg_keys[0], (SNAPSHOT_COUNT, V, F), 1.0, 6.0, ((0, 16), (1, 32))),
        "tile_src": draw_tile_src(jax.random.fold_in(arg_keys[14], 71), 0),
        "tile_dst": draw_tile_dst(jax.random.fold_in(arg_keys[14], 71), 0),
        "tile_count": draw_tile_count(jax.random.fold_in(arg_keys[14], 71), 0),
        "tile_vals": gaussian(arg_keys[4], (SNAPSHOT_COUNT, N_VERT * TILE_CAP, TILE, TILE), (TILE * TILE_CAP // (2 * BPD)) ** -0.5, 0.25, ((0, 16), (1, 32))),
        "norm_gain": jnp.clip(1.0 + 0.15 * jax.random.normal(arg_keys[5], (F,), jnp.float32), 0.25, 1.75),
        "mix_weight": gaussian(arg_keys[6], (F, 2 * F), F ** -0.5, 0.375),
        "decay_rate": draw_decay_rate(jax.random.fold_in(arg_keys[14], 71), 0),
        "mlp_gain": jnp.clip(1.0 + 0.15 * jax.random.normal(arg_keys[8], (F,), jnp.float32), 0.25, 1.75),
        "up_weight": gaussian(arg_keys[9], (F, HID), F ** -0.5, 0.375),
        "down_weight": gaussian(arg_keys[10], (HID, F), HID ** -0.5, 0.1875),
        "link_weight": gaussian(arg_keys[11], (F, F), F ** -0.5, 0.375),
        "pair_left": draw_pair_left(jax.random.fold_in(arg_keys[14], 71), 0),
        "pair_right": draw_pair_right(jax.random.fold_in(arg_keys[14], 71), 0),
    }


epsilon = 1e-06

def root_norm(values, gain_vector):
    return values * lax.rsqrt(lax.optimization_barrier(jnp.mean(values * values, axis=-1, keepdims=True)) + epsilon) * gain_vector

def advance(previous, inputs):
    updated = inputs[0] * previous + inputs[1]
    return (updated, updated)

def reference(features, tile_src, tile_dst, tile_count, tile_vals, norm_gain, mix_weight, decay_rate, mlp_gain, up_weight, down_weight, link_weight, pair_left, pair_right):
    slot_ids = jnp.arange(TILE_CAP, dtype=jnp.int32)

    def aggregate_one(inputs):
        snapshot, sources, targets, counts, tiles = inputs
        picked = snapshot.reshape(NB, TILE, F)[sources].astype(jnp.float32)
        product = jnp.einsum('kij,kjf->kif', tiles.astype(jnp.float32), picked)
        alive_slots = (slot_ids[None, :] < counts[:, None]).reshape(-1)
        product = product * alive_slots[:, None, None].astype(jnp.float32)
        summed = jax.ops.segment_sum(product, targets, num_segments=NB)
        return summed.reshape(V, F)
    aggregate = lax.map(aggregate_one, (features, tile_src, tile_dst, tile_count, tile_vals))
    normed = root_norm(aggregate + features.astype(jnp.float32), norm_gain).astype(jnp.bfloat16)
    projected = jnp.einsum('tnf,fg->tng', normed.astype(jnp.float32), mix_weight.astype(jnp.float32))
    decays = jnp.exp(-decay_rate[:, None, :] * jax.nn.sigmoid(projected[..., :F]))
    drives = (1.0 - decays) * projected[..., F:]
    final_state, states = lax.scan(advance, jnp.zeros((V, F), jnp.float32), (decays, drives))
    state_normed = root_norm(states, mlp_gain).astype(jnp.bfloat16)
    hidden = jax.nn.silu(jnp.einsum('tnf,fh->tnh', state_normed.astype(jnp.float32), up_weight.astype(jnp.float32))).astype(jnp.bfloat16)
    embeddings = (states + jnp.einsum('tnh,hf->tnf', hidden.astype(jnp.float32), down_weight.astype(jnp.float32))).astype(jnp.bfloat16)
    left_side = jnp.einsum('tnf,fg->tng', embeddings.astype(jnp.float32), link_weight.astype(jnp.float32)).astype(jnp.bfloat16)
    scale_factor = F ** (-0.5)

    def score_one(inputs):
        left_rows, right_rows, left_index, right_index = inputs
        left_blocks = left_rows.reshape(NB, TILE, F)[left_index].astype(jnp.float32)
        right_blocks = right_rows.reshape(NB, TILE, F)[right_index].astype(jnp.float32)
        tiles_out = jnp.einsum('pif,pjf->pij', left_blocks, right_blocks) * scale_factor
        return tiles_out.astype(jnp.bfloat16)
    scores = lax.map(score_one, (left_side, embeddings, pair_left, pair_right))
    return (embeddings, scores)
```

```python
import functools

import jax
import jax.numpy as jnp
from jax import lax
from jax.experimental import pallas as pl
from jax.experimental.pallas import tpu as pltpu
from jax.sharding import PartitionSpec as P

epsilon = 1e-06
VMEM = pl.BlockSpec(memory_space=pltpu.VMEM)
SMEM = pl.BlockSpec(memory_space=pltpu.SMEM)


def call(kernel, outs, in_specs, flops, bytes_accessed, transcendentals=0, scratch=()):
    return pl.pallas_call(
        kernel,
        out_shape=outs,
        in_specs=in_specs,
        out_specs=jax.tree.map(lambda _: VMEM, outs),
        scratch_shapes=list(scratch),
        compiler_params=pltpu.CompilerParams(vmem_limit_bytes=40 * 2**20),
        cost_estimate=pl.CostEstimate(
            flops=flops, bytes_accessed=bytes_accessed, transcendentals=transcendentals
        ),
    )


def block_rows(index, rows):
    return pl.ds(pl.multiple_of(index * rows, rows), rows)


def aggregate_kernel(
    per_part, src, dst, count, own, below, above, tiles, gain, normed, blocks, total
):
    slots, rows, _ = tiles.shape
    vertices = own.shape[0]
    blocks[:vertices] = below[...]
    blocks[vertices : 2 * vertices] = own[...]
    blocks[2 * vertices :] = above[...]
    total[...] = own[...].astype(jnp.float32)
    live = count[0, 0]
    for k in range(slots):
        target = dst[0, k]
        local = lax.rem(target, per_part)
        source = src[0, k] - (target - local) + per_part
        tile = jnp.where(k < live, tiles[k], jnp.zeros((), tiles.dtype))
        total[block_rows(local, rows)] += jnp.dot(
            tile, blocks[block_rows(source, rows)], preferred_element_type=jnp.float32
        )
    combined = total[...]
    scale = lax.rsqrt(jnp.mean(combined * combined, axis=-1, keepdims=True) + epsilon)
    normed[...] = (combined * scale * gain[...]).astype(normed.dtype)


def vertex_kernel(normed, mix, rates, gain, up, down, out):
    steps, rows, width = normed.shape
    state = jnp.zeros((rows, width), jnp.float32)
    group = 4
    for first in range(0, steps, group):
        projected = jnp.dot(
            normed[first : first + group].reshape(group * rows, width),
            mix[...],
            preferred_element_type=jnp.float32,
        )
        gate = 1.0 / (1.0 + jnp.exp(-projected[:, :width]))
        states = []
        for j in range(group):
            part = slice(j * rows, (j + 1) * rows)
            decays = jnp.exp(-rates[first + j : first + j + 1] * gate[part])
            state = decays * state + (1.0 - decays) * projected[part, width:]
            states.append(state)
        states = jnp.concatenate(states)
        scale = lax.rsqrt(jnp.mean(states * states, axis=-1, keepdims=True) + epsilon)
        state_normed = (states * scale * gain[...]).astype(jnp.bfloat16)
        inner = jnp.dot(state_normed, up[...], preferred_element_type=jnp.float32)
        hidden = (inner / (1.0 + jnp.exp(-inner))).astype(jnp.bfloat16)
        result = states + jnp.dot(hidden, down[...], preferred_element_type=jnp.float32)
        out[first : first + group] = result.astype(out.dtype).reshape(group, rows, width)


def left_kernel(embeddings, link, left):
    left[...] = jnp.dot(
        embeddings[...], link[...], preferred_element_type=jnp.float32
    ).astype(left.dtype)


def score_kernel(per_part, pair_left, pair_right, left, own, below, above, scores, blocks):
    pairs, rows, _ = scores.shape
    vertices, width = own.shape
    blocks[:vertices] = below[...]
    blocks[vertices : 2 * vertices] = own[...]
    blocks[2 * vertices :] = above[...]
    for k in range(pairs):
        first = pair_left[0, k]
        local = lax.rem(first, per_part)
        other = pair_right[0, k] - (first - local) + per_part
        product = lax.dot_general(
            left[block_rows(local, rows)],
            blocks[block_rows(other, rows)],
            (((1,), (1,)), ((), ())),
            preferred_element_type=jnp.float32,
        )
        scores[k] = (product * width**-0.5).astype(scores.dtype)


def ring_halo(cells):
    count = lax.axis_size("vert")
    below = lax.ppermute(cells, "vert", [(i, (i + 1) % count) for i in range(count)])
    above = lax.ppermute(cells, "vert", [((i + 1) % count, i) for i in range(count)])
    return below, above


def body(
    features,
    tile_src,
    tile_dst,
    tile_count,
    tile_vals,
    norm_gain,
    mix_weight,
    decay_rate,
    mlp_gain,
    up_weight,
    down_weight,
    link_weight,
    pair_left,
    pair_right,
):
    _, vertices, width = features.shape
    _, slots, rows, _ = tile_vals.shape
    pairs = pair_left.shape[1]
    per_part = vertices // rows
    snaps = lax.axis_size("snap")
    hidden = up_weight.shape[1]
    bf16 = jnp.bfloat16
    own = features.reshape(vertices, width)
    below, above = ring_halo(own)
    normed = call(
        functools.partial(aggregate_kernel, per_part),
        jax.ShapeDtypeStruct((vertices, width), bf16),
        [SMEM, SMEM, SMEM, VMEM, VMEM, VMEM, VMEM, VMEM],
        2 * slots * rows * rows * width,
        2 * slots * rows * rows,
        scratch=[
            pltpu.VMEM((3 * vertices, width), bf16),
            pltpu.VMEM((vertices, width), jnp.float32),
        ],
    )(
        tile_src,
        tile_dst,
        tile_count,
        own,
        below,
        above,
        tile_vals.reshape(slots, rows, rows),
        norm_gain.reshape(1, width),
    )
    by_vertex = lax.all_to_all(
        normed.reshape(snaps, vertices // snaps, width), "snap", 0, 0, tiled=True
    )
    vertex_out = call(
        vertex_kernel,
        jax.ShapeDtypeStruct(by_vertex.shape, bf16),
        [VMEM] * 6,
        2 * vertices * width * (2 * width + 2 * hidden),
        4 * width * (width + hidden),
        vertices * (2 * width + hidden),
    )(
        by_vertex,
        mix_weight,
        decay_rate,
        mlp_gain.reshape(1, width),
        up_weight,
        down_weight,
    )
    embeddings = lax.all_to_all(vertex_out, "snap", 0, 0, tiled=True).reshape(
        vertices, width
    )
    below_out, above_out = ring_halo(embeddings)
    left = call(
        left_kernel,
        jax.ShapeDtypeStruct((vertices, width), bf16),
        [VMEM] * 2,
        2 * vertices * width * width,
        4 * vertices * width,
    )(embeddings, link_weight)
    scores = call(
        functools.partial(score_kernel, per_part),
        jax.ShapeDtypeStruct((pairs, rows, rows), bf16),
        [SMEM, SMEM, VMEM, VMEM, VMEM, VMEM],
        2 * pairs * rows * rows * width,
        2 * pairs * rows * rows,
        scratch=[pltpu.VMEM((3 * vertices, width), bf16)],
    )(pair_left, pair_right, left, embeddings, below_out, above_out)
    return (
        embeddings.reshape(1, vertices, width),
        scores.reshape(1, pairs, rows, rows),
    )


def solution(mesh):
    return jax.shard_map(
        body,
        mesh=mesh,
        in_specs=(
            P("snap", "vert", None),
            P("snap", "vert"),
            P("snap", "vert"),
            P("snap", "vert"),
            P("snap", "vert", None, None),
            P(),
            P(),
            P(),
            P(),
            P(),
            P(),
            P(),
            P("snap", "vert"),
            P("snap", "vert"),
        ),
        out_specs=(P("snap", "vert", None), P("snap", "vert", None, None)),
        check_vma=False,
    )
```

```python
import functools

import jax
import jax.numpy as jnp
from jax import lax
from jax.experimental import pallas as pl
from jax.experimental.pallas import tpu as pltpu
from jax.sharding import PartitionSpec as P

epsilon = 1e-06
VMEM = pl.BlockSpec(memory_space=pltpu.VMEM)
SMEM = pl.BlockSpec(memory_space=pltpu.SMEM)


ANY = pl.BlockSpec(memory_space=pl.ANY)
HBM = pl.BlockSpec(memory_space=pltpu.HBM)


def call(kernel, outs, out_specs, in_specs, cost, scratch=()):
    flops, bytes_accessed, transcendentals = cost
    return pl.pallas_call(
        kernel,
        out_shape=outs,
        in_specs=in_specs,
        out_specs=out_specs,
        scratch_shapes=list(scratch),
        compiler_params=pltpu.CompilerParams(vmem_limit_bytes=40 * 2**20),
        cost_estimate=pl.CostEstimate(
            flops=flops, bytes_accessed=bytes_accessed, transcendentals=transcendentals
        ),
    )


def block_rows(index, rows):
    return pl.ds(pl.multiple_of(index * rows, rows), rows)


def prepare_kernel(
    per_part,
    src,
    dst,
    count,
    pair_left,
    pair_right,
    own,
    tiles,
    norm_gain,
    mlp_gain,
    tile_index,
    pair_index,
    own_out,
    tiles_out,
    norm_gain_out,
    mlp_gain_out,
    sems,
):
    moves = [
        pltpu.make_async_copy(source, target, sems.at[i])
        for i, (source, target) in enumerate(
            (
                (tiles, tiles_out),
                (own, own_out),
                (norm_gain, norm_gain_out),
                (mlp_gain, mlp_gain_out),
            )
        )
    ]
    for move in moves:
        move.start()
    slots = tiles.shape[0]
    for k in range(slots):
        local = lax.rem(dst[0, k], per_part)
        tile_index[0, k] = local
        tile_index[1, k] = src[0, k] - (dst[0, k] - local) + per_part
    for k in range(pair_left.shape[1]):
        local = lax.rem(pair_left[0, k], per_part)
        pair_index[0, k] = local
        pair_index[1, k] = pair_right[0, k] - (pair_left[0, k] - local) + per_part
    for move in moves:
        move.wait()

    @pl.loop(count[0, 0], slots)
    def _(k):
        tiles_out[k] = jnp.zeros_like(tiles_out[k])


def aggregate_kernel(index, own, below, above, tiles, gain, normed, blocks, even, odd):
    slots, rows, _ = tiles.shape
    vertices = own.shape[0]
    blocks[:vertices] = below[...]
    blocks[vertices : 2 * vertices] = own[...]
    blocks[2 * vertices :] = above[...]
    even[...] = own[...].astype(jnp.float32)
    odd[...] = jnp.zeros_like(odd)
    for k in range(slots):
        total = odd if k % 2 else even
        total[block_rows(index[0, k], rows)] += jnp.dot(
            tiles[k],
            blocks[block_rows(index[1, k], rows)],
            preferred_element_type=jnp.float32,
        )
    combined = even[...] + odd[...]
    scale = lax.rsqrt(jnp.mean(combined * combined, axis=-1, keepdims=True) + epsilon)
    normed[...] = (combined * scale * gain[...]).astype(normed.dtype)


def vertex_kernel(normed, mix, rates, gain, up, down, out):
    steps, rows, width = normed.shape
    projected = jnp.dot(
        normed[...].reshape(steps * rows, width),
        mix[...],
        preferred_element_type=jnp.float32,
    )
    gate = 1.0 / (1.0 + jnp.exp(-projected[:, :width]))
    state = jnp.zeros((rows, width), jnp.float32)
    states = []
    for step in range(steps):
        part = slice(step * rows, (step + 1) * rows)
        decays = jnp.exp(-rates[step : step + 1] * gate[part])
        state = decays * state + (1.0 - decays) * projected[part, width:]
        states.append(state)
    states = jnp.concatenate(states)
    scale = lax.rsqrt(jnp.mean(states * states, axis=-1, keepdims=True) + epsilon)
    state_normed = (states * scale * gain[...]).astype(jnp.bfloat16)
    inner = jnp.dot(state_normed, up[...], preferred_element_type=jnp.float32)
    hidden = (inner / (1.0 + jnp.exp(-inner))).astype(jnp.bfloat16)
    result = states + jnp.dot(hidden, down[...], preferred_element_type=jnp.float32)
    out[...] = result.astype(out.dtype).reshape(steps, rows, width)


def left_kernel(embeddings, link, left, kept, sem):
    keep = pltpu.make_async_copy(embeddings, kept, sem)
    keep.start()
    left[...] = jnp.dot(
        embeddings[...], link[...], preferred_element_type=jnp.float32
    ).astype(left.dtype)
    keep.wait()


def score_kernel(index, left, own, below, above, scores, blocks, tiles, sems):
    pairs, rows, _ = scores.shape
    vertices, width = own.shape
    blocks[:vertices] = below[...]
    blocks[vertices : 2 * vertices] = own[...]
    blocks[2 * vertices :] = above[...]
    batch = pairs // sems.shape[0]
    moves = []
    for k in range(pairs):
        product = lax.dot_general(
            left[block_rows(index[0, k], rows)],
            blocks[block_rows(index[1, k], rows)],
            (((1,), (1,)), ((), ())),
            preferred_element_type=jnp.float32,
        )
        tiles[k] = (product * width**-0.5).astype(tiles.dtype)
        if (k + 1) % batch == 0:
            part = pl.ds(k + 1 - batch, batch)
            moves.append(
                pltpu.make_async_copy(tiles.at[part], scores.at[part], sems.at[k // batch])
            )
            moves[-1].start()
    for move in moves:
        move.wait()


def ring_halo(cells):
    count = lax.axis_size("vert")
    below = lax.ppermute(cells, "vert", [(i, (i + 1) % count) for i in range(count)])
    above = lax.ppermute(cells, "vert", [((i + 1) % count, i) for i in range(count)])
    return below, above


def body(
    features,
    tile_src,
    tile_dst,
    tile_count,
    tile_vals,
    norm_gain,
    mix_weight,
    decay_rate,
    mlp_gain,
    up_weight,
    down_weight,
    link_weight,
    pair_left,
    pair_right,
):
    _, vertices, width = features.shape
    _, slots, rows, _ = tile_vals.shape
    pairs = pair_left.shape[1]
    per_part = vertices // rows
    snaps = lax.axis_size("snap")
    hidden = up_weight.shape[1]
    bf16 = jnp.bfloat16
    f32 = jnp.float32
    shape = jax.ShapeDtypeStruct
    own = features.reshape(vertices, width)
    below, above = ring_halo(own)
    tile_index, pair_index, own_near, tiles, norm_row, mlp_row = call(
        functools.partial(prepare_kernel, per_part),
        (
            shape((2, slots), jnp.int32),
            shape((2, pairs), jnp.int32),
            shape((vertices, width), bf16),
            shape((slots, rows, rows), bf16),
            shape((1, width), f32),
            shape((1, width), f32),
        ),
        (SMEM, SMEM, VMEM, VMEM, VMEM, VMEM),
        [SMEM] * 5 + [HBM] * 4,
        (0, 4 * slots * rows * rows, 0),
        [pltpu.SemaphoreType.DMA((4,))],
    )(
        tile_src,
        tile_dst,
        tile_count,
        pair_left,
        pair_right,
        own,
        tile_vals.reshape(slots, rows, rows),
        norm_gain.reshape(1, width),
        mlp_gain.reshape(1, width),
    )
    normed = call(
        aggregate_kernel,
        shape((vertices, width), bf16),
        VMEM,
        [SMEM] + [VMEM] * 5,
        (2 * slots * rows * rows * width, 2 * slots * rows * rows, 0),
        [
            pltpu.VMEM((3 * vertices, width), bf16),
            pltpu.VMEM((vertices, width), f32),
            pltpu.VMEM((vertices, width), f32),
        ],
    )(tile_index, own_near, below, above, tiles, norm_row)
    by_vertex = lax.all_to_all(
        normed.reshape(snaps, vertices // snaps, width), "snap", 0, 0, tiled=True
    )
    vertex_out = call(
        vertex_kernel,
        shape(by_vertex.shape, bf16),
        VMEM,
        [VMEM] * 6,
        (
            2 * vertices * width * (2 * width + 2 * hidden),
            4 * width * (width + hidden),
            vertices * (2 * width + hidden),
        ),
    )(by_vertex, mix_weight, decay_rate, mlp_row, up_weight, down_weight)
    embeddings = lax.all_to_all(vertex_out, "snap", 0, 0, tiled=True).reshape(
        vertices, width
    )
    below_out, above_out = ring_halo(embeddings)
    left, kept = call(
        left_kernel,
        (shape((vertices, width), bf16), shape((vertices, width), bf16)),
        (VMEM, ANY),
        [VMEM] * 2,
        (2 * vertices * width * width, 8 * vertices * width, 0),
        [pltpu.SemaphoreType.DMA],
    )(embeddings, link_weight)
    scores = call(
        score_kernel,
        shape((pairs, rows, rows), bf16),
        ANY,
        [SMEM] + [VMEM] * 4,
        (2 * pairs * rows * rows * width, 2 * pairs * rows * rows, 0),
        [
            pltpu.VMEM((3 * vertices, width), bf16),
            pltpu.VMEM((pairs, rows, rows), bf16),
            pltpu.SemaphoreType.DMA((8,)),
        ],
    )(pair_index, left, embeddings, below_out, above_out)
    return (
        kept.reshape(1, vertices, width),
        scores.reshape(1, pairs, rows, rows),
    )


def solution(mesh):
    return jax.shard_map(
        body,
        mesh=mesh,
        in_specs=(
            P("snap", "vert", None),
            P("snap", "vert"),
            P("snap", "vert"),
            P("snap", "vert"),
            P("snap", "vert", None, None),
            P(),
            P(),
            P(),
            P(),
            P(),
            P(),
            P(),
            P("snap", "vert"),
            P("snap", "vert"),
        ),
        out_specs=(P("snap", "vert", None), P("snap", "vert", None, None)),
        check_vma=False,
    )
```

```python
import functools

import jax
import jax.numpy as jnp
from jax import lax
from jax.experimental import pallas as pl
from jax.experimental.pallas import tpu as pltpu
from jax.sharding import PartitionSpec as P

epsilon = 1e-06
VMEM = pl.BlockSpec(memory_space=pltpu.VMEM)
SMEM = pl.BlockSpec(memory_space=pltpu.SMEM)


ANY = pl.BlockSpec(memory_space=pl.ANY)
HBM = pl.BlockSpec(memory_space=pltpu.HBM)


def call(kernel, outs, out_specs, in_specs, cost, scratch=()):
    flops, bytes_accessed, transcendentals = cost
    return pl.pallas_call(
        kernel,
        out_shape=outs,
        in_specs=in_specs,
        out_specs=out_specs,
        scratch_shapes=list(scratch),
        compiler_params=pltpu.CompilerParams(vmem_limit_bytes=40 * 2**20),
        cost_estimate=pl.CostEstimate(
            flops=flops, bytes_accessed=bytes_accessed, transcendentals=transcendentals
        ),
    )


def block_rows(index, rows):
    return pl.ds(pl.multiple_of(index * rows, rows), rows)


def near(own_block, other_block, per_part):
    first = own_block - lax.rem(own_block, 2 * per_part)
    other = lax.rem(other_block - first + 3 * per_part, 3 * per_part)
    return lax.rem(own_block, per_part), other


def add_tile(totals, order, index, tiles, blocks, slot, keep):
    rows = tiles.shape[1]
    tile = jnp.where(keep, tiles[slot], jnp.zeros((), tiles.dtype))
    totals[order % 2][block_rows(index[0, slot], rows)] += jnp.dot(
        tile,
        blocks[block_rows(index[1, slot], rows)],
        preferred_element_type=jnp.float32,
    )


def prepare_kernel(
    per_part,
    count,
    src,
    dst,
    pair_left,
    pair_right,
    norm_gain,
    mlp_gain,
    tiles,
    tile_index,
    pair_index,
    norm_gain_out,
    mlp_gain_out,
    tiles_out,
    src_near,
    dst_near,
    left_near,
    right_near,
    sems,
):
    lists = (
        (src, src_near),
        (dst, dst_near),
        (pair_left, left_near),
        (pair_right, right_near),
    )
    arrays = (
        (tiles, tiles_out),
        (norm_gain, norm_gain_out),
        (mlp_gain, mlp_gain_out),
    )
    moves = [
        pltpu.make_async_copy(source, target, sems.at[i])
        for i, (source, target) in enumerate(lists + arrays)
    ]
    for move in moves:
        move.start()
    for move in moves[: len(lists)]:
        move.wait()
    for k in range(src.shape[1]):
        tile_index[0, k], tile_index[1, k] = near(
            dst_near[0, k], src_near[0, k], per_part
        )
    tile_index[2, 0] = count[0, 0]
    for k in range(pair_left.shape[1]):
        pair_index[0, k], pair_index[1, k] = near(
            left_near[0, k], right_near[0, k], per_part
        )
    for move in moves[len(lists) :]:
        move.wait()


def aggregate_kernel(core, index, pair, halo, tiles, gain, normed, blocks, even, odd):
    slots, rows, _ = tiles.shape
    vertices = halo.shape[0]
    blocks[: 2 * vertices] = pair[...]
    blocks[2 * vertices :] = halo[...]
    even[...] = pair[block_rows(core[0], vertices)].astype(jnp.float32)
    odd[...] = jnp.zeros_like(odd)
    live = index[2, 0]
    for k in range(slots):
        add_tile((even, odd), k, index, tiles, blocks, k, k < live)
    combined = even[...] + odd[...]
    scale = lax.rsqrt(jnp.mean(combined * combined, axis=-1, keepdims=True) + epsilon)
    normed[...] = (combined * scale * gain[...]).astype(normed.dtype)


def vertex_kernel(normed, mix, rates, gain, up, down, out):
    steps, rows, width = normed.shape
    projected = jnp.dot(
        normed[...].reshape(steps * rows, width),
        mix[...],
        preferred_element_type=jnp.float32,
    )
    gate = 1.0 / (1.0 + jnp.exp(-projected[:, :width]))
    state = jnp.zeros((rows, width), jnp.float32)
    states = []
    for step in range(steps):
        part = slice(step * rows, (step + 1) * rows)
        decays = jnp.exp(-rates[step : step + 1] * gate[part])
        state = decays * state + (1.0 - decays) * projected[part, width:]
        states.append(state)
    states = jnp.concatenate(states)
    scale = lax.rsqrt(jnp.mean(states * states, axis=-1, keepdims=True) + epsilon)
    state_normed = (states * scale * gain[...]).astype(jnp.bfloat16)
    inner = jnp.dot(state_normed, up[...], preferred_element_type=jnp.float32)
    hidden = (inner / (1.0 + jnp.exp(-inner))).astype(jnp.bfloat16)
    result = states + jnp.dot(hidden, down[...], preferred_element_type=jnp.float32)
    out[...] = result.astype(out.dtype).reshape(steps, rows, width)


def left_kernel(embeddings, link, left, kept, sem):
    keep = pltpu.make_async_copy(embeddings, kept, sem)
    keep.start()
    left[...] = jnp.dot(
        embeddings[...], link[...], preferred_element_type=jnp.float32
    ).astype(left.dtype)
    keep.wait()


def score_kernel(index, left, pair, halo, scores, blocks, tiles, sems):
    pairs, rows, _ = scores.shape
    vertices, width = halo.shape
    blocks[: 2 * vertices] = pair[...]
    blocks[2 * vertices :] = halo[...]
    batch = pairs // sems.shape[0]
    moves = []
    for k in range(pairs):
        product = lax.dot_general(
            left[block_rows(index[0, k], rows)],
            blocks[block_rows(index[1, k], rows)],
            (((1,), (1,)), ((), ())),
            preferred_element_type=jnp.float32,
        )
        tiles[k] = (product * width**-0.5).astype(tiles.dtype)
        if (k + 1) % batch == 0:
            part = pl.ds(k + 1 - batch, batch)
            moves.append(
                pltpu.make_async_copy(tiles.at[part], scores.at[part], sems.at[k // batch])
            )
            moves[-1].start()
    for move in moves:
        move.wait()


def chip_halo(cells):
    count = lax.axis_size("vert")
    links = [(i, i + 1) for i in range(1, count - 1, 2)]
    halo = lax.ppermute(cells, "vert", links + [(j, i) for i, j in links])
    chips = [[i, i + 1] for i in range(0, count, 2)]
    pair = lax.all_gather(cells, "vert", axis_index_groups=chips, tiled=True)
    return pair, halo


def body(
    features,
    tile_src,
    tile_dst,
    tile_count,
    tile_vals,
    norm_gain,
    mix_weight,
    decay_rate,
    mlp_gain,
    up_weight,
    down_weight,
    link_weight,
    pair_left,
    pair_right,
):
    _, vertices, width = features.shape
    _, slots, rows, _ = tile_vals.shape
    pairs = pair_left.shape[1]
    per_part = vertices // rows
    snaps = lax.axis_size("snap")
    hidden = up_weight.shape[1]
    bf16 = jnp.bfloat16
    f32 = jnp.float32
    shape = jax.ShapeDtypeStruct
    own = features.reshape(vertices, width)
    core = lax.rem(lax.axis_index("vert"), 2).astype(jnp.int32).reshape(1)
    pair, halo = chip_halo(own)
    tile_index, pair_index, norm_row, mlp_row, tiles = call(
        functools.partial(prepare_kernel, per_part),
        (
            shape((3, slots), jnp.int32),
            shape((2, pairs), jnp.int32),
            shape((1, width), f32),
            shape((1, width), f32),
            shape((slots, rows, rows), bf16),
        ),
        (SMEM, SMEM, VMEM, VMEM, VMEM),
        [SMEM] + [HBM] * 7,
        (0, 4 * slots * rows * rows, 0),
        [
            pltpu.SMEM((1, slots), jnp.int32),
            pltpu.SMEM((1, slots), jnp.int32),
            pltpu.SMEM((1, pairs), jnp.int32),
            pltpu.SMEM((1, pairs), jnp.int32),
            pltpu.SemaphoreType.DMA((7,)),
        ],
    )(
        tile_count,
        *[
            pltpu.with_memory_space_constraint(x, pltpu.HBM)
            for x in (
                tile_src,
                tile_dst,
                pair_left,
                pair_right,
                norm_gain.reshape(1, width),
                mlp_gain.reshape(1, width),
                tile_vals.reshape(slots, rows, rows),
            )
        ]
    )
    normed = call(
        aggregate_kernel,
        shape((vertices, width), bf16),
        VMEM,
        [SMEM] * 2 + [VMEM] * 4,
        (2 * slots * rows * rows * width, 2 * slots * rows * rows, 0),
        [
            pltpu.VMEM((3 * vertices, width), bf16),
            pltpu.VMEM((vertices, width), f32),
            pltpu.VMEM((vertices, width), f32),
        ],
    )(core, tile_index, pair, halo, tiles, norm_row)
    by_vertex = lax.all_to_all(
        normed.reshape(snaps, vertices // snaps, width), "snap", 0, 0, tiled=True
    )
    vertex_out = call(
        vertex_kernel,
        shape(by_vertex.shape, bf16),
        VMEM,
        [VMEM] * 6,
        (
            2 * vertices * width * (2 * width + 2 * hidden),
            4 * width * (width + hidden),
            vertices * (2 * width + hidden),
        ),
    )(by_vertex, mix_weight, decay_rate, mlp_row, up_weight, down_weight)
    embeddings = lax.all_to_all(vertex_out, "snap", 0, 0, tiled=True).reshape(
        vertices, width
    )
    pair_out, halo_out = chip_halo(embeddings)
    left, kept = call(
        left_kernel,
        (shape((vertices, width), bf16), shape((vertices, width), bf16)),
        (VMEM, ANY),
        [VMEM] * 2,
        (2 * vertices * width * width, 8 * vertices * width, 0),
        [pltpu.SemaphoreType.DMA],
    )(embeddings, link_weight)
    scores = call(
        score_kernel,
        shape((pairs, rows, rows), bf16),
        ANY,
        [SMEM] + [VMEM] * 3,
        (2 * pairs * rows * rows * width, 2 * pairs * rows * rows, 0),
        [
            pltpu.VMEM((3 * vertices, width), bf16),
            pltpu.VMEM((pairs, rows, rows), bf16),
            pltpu.SemaphoreType.DMA((8,)),
        ],
    )(pair_index, left, pair_out, halo_out)
    return (
        kept.reshape(1, vertices, width),
        scores.reshape(1, pairs, rows, rows),
    )


def solution(mesh):
    return jax.shard_map(
        body,
        mesh=mesh,
        in_specs=(
            P("snap", "vert", None),
            P("snap", "vert"),
            P("snap", "vert"),
            P("snap", "vert"),
            P("snap", "vert", None, None),
            P(),
            P(),
            P(),
            P(),
            P(),
            P(),
            P(),
            P("snap", "vert"),
            P("snap", "vert"),
        ),
        out_specs=(P("snap", "vert", None), P("snap", "vert", None, None)),
        check_vma=False,
    )
```

```python
import functools

import jax
import jax.numpy as jnp
from jax import lax
from jax.experimental import pallas as pl
from jax.experimental.pallas import tpu as pltpu
from jax.sharding import PartitionSpec as P

epsilon = 1e-06
list_rows = 16
VMEM = pl.BlockSpec(memory_space=pltpu.VMEM)
SMEM = pl.BlockSpec(memory_space=pltpu.SMEM)


ANY = pl.BlockSpec(memory_space=pl.ANY)
HBM = pl.BlockSpec(memory_space=pltpu.HBM)


def call(kernel, outs, out_specs, in_specs, cost, scratch=()):
    flops, bytes_accessed, transcendentals = cost
    return pl.pallas_call(
        kernel,
        out_shape=outs,
        in_specs=in_specs,
        out_specs=out_specs,
        scratch_shapes=list(scratch),
        compiler_params=pltpu.CompilerParams(vmem_limit_bytes=40 * 2**20),
        cost_estimate=pl.CostEstimate(
            flops=flops, bytes_accessed=bytes_accessed, transcendentals=transcendentals
        ),
    )


def block_rows(index, rows):
    return pl.ds(pl.multiple_of(index * rows, rows), rows)


def near(own_block, other_block, per_part):
    other = other_block - (own_block & -(2 * per_part)) + 3 * per_part
    other = jnp.where(other >= 3 * per_part, other - 3 * per_part, other)
    return own_block & (per_part - 1), other


def core_index():
    return lax.rem(lax.axis_index("vert"), 2)


def prepare_kernel(count, src, dst, own, joined, src_near, dst_near, row, sems):
    vertices, width = own.shape
    slots = src.shape[1]
    lanes = width // 2
    row[...] = jnp.full(row.shape, count[0, 0], jnp.int32)
    moves = [
        pltpu.make_async_copy(source, target, sems.at[i])
        for i, (source, target) in enumerate(
            ((src, src_near), (dst, dst_near), (own, joined.at[:vertices]))
        )
    ]
    for move in moves:
        move.start()
    for move in moves[:2]:
        move.wait()
    row[:, :slots] = src_near[...]
    row[:, lanes : lanes + slots] = dst_near[...]
    trailer = row[...].astype(jnp.float32).astype(joined.dtype)
    joined[vertices:] = jnp.broadcast_to(trailer, (list_rows, width))
    moves[2].wait()


def blocks_kernel(
    per_part, gain, out_gain, pair, halo, blocks, lists, own, gain_near, out_gain_near, sems
):
    vertices, width = halo.shape
    stride = pair.shape[0] // 2
    mate = 1 - core_index()
    loads = [
        pltpu.make_async_copy(gain, gain_near, sems.at[0]),
        pltpu.make_async_copy(out_gain, out_gain_near, sems.at[1]),
    ]
    for load in loads:
        load.start()
    place = pl.multiple_of(mate * stride, list_rows)
    start = pl.multiple_of(mate * stride + vertices, list_rows)
    trailer = pair[pl.ds(start, list_rows)].astype(jnp.float32)[:1].astype(jnp.int32)
    lanes = width // 2
    lists[0:1], lists[1:2] = near(trailer[:, lanes:], trailer[:, :lanes], per_part)
    lists[2:3] = trailer[:, :lanes]
    blocks[:vertices] = pair[:vertices]
    blocks[vertices : 2 * vertices] = pair[stride : stride + vertices]
    blocks[2 * vertices :] = halo[...]
    own[...] = pair[pl.ds(place, vertices)].astype(jnp.float32)
    for load in loads:
        load.wait()


def aggregate_kernel(lists, blocks, own, gain, tiles, normed, even, odd, index, sem):
    slots, rows, _ = tiles.shape
    fetch = pltpu.make_async_copy(lists, index, sem)
    fetch.start()
    even[...] = own[...]
    odd[...] = jnp.zeros_like(odd)
    fetch.wait()
    live = index[2, slots]
    for k in range(slots):
        total = odd if k % 2 else even
        total[block_rows(index[0, k], rows)] += jnp.dot(
            jnp.where(k < live, tiles[k], jnp.zeros((), tiles.dtype)),
            blocks[block_rows(index[1, k], rows)],
            preferred_element_type=jnp.float32,
        )
    combined = even[...] + odd[...]
    scale = lax.rsqrt(jnp.mean(combined * combined, axis=-1, keepdims=True) + epsilon)
    normed[...] = (combined * scale * gain[...]).astype(normed.dtype)


def vertex_kernel(gain, normed, mix, rates, up, down, out):
    steps, rows, width = normed.shape
    projected = jnp.dot(
        normed[...].reshape(steps * rows, width),
        mix[...],
        preferred_element_type=jnp.float32,
    )
    gate = 1.0 / (1.0 + jnp.exp(-projected[:, :width]))
    state = jnp.zeros((rows, width), jnp.float32)
    states = []
    for step in range(steps):
        part = slice(step * rows, (step + 1) * rows)
        decays = jnp.exp(-rates[step : step + 1] * gate[part])
        state = decays * state + (1.0 - decays) * projected[part, width:]
        states.append(state)
    states = jnp.concatenate(states)
    scale = lax.rsqrt(jnp.mean(states * states, axis=-1, keepdims=True) + epsilon)
    state_normed = (states * scale * gain[...]).astype(jnp.bfloat16)
    inner = jnp.dot(state_normed, up[...], preferred_element_type=jnp.float32)
    hidden = (inner / (1.0 + jnp.exp(-inner))).astype(jnp.bfloat16)
    result = states + jnp.dot(hidden, down[...], preferred_element_type=jnp.float32)
    out[...] = result.astype(out.dtype).reshape(steps, rows, width)


def left_kernel(
    per_part, pair_left, pair_right, pair, link, left, kept, lists, left_near, right_near, sems
):
    own = block_rows(1 - core_index(), left.shape[0])
    moves = [
        pltpu.make_async_copy(source, target, sems.at[i])
        for i, (source, target) in enumerate(
            ((pair_left, left_near), (pair_right, right_near), (pair.at[own], kept))
        )
    ]
    for move in moves:
        move.start()
    left[...] = jnp.dot(
        pair[own], link[...], preferred_element_type=jnp.float32
    ).astype(left.dtype)
    for move in moves[:2]:
        move.wait()
    pairs = left_near.shape[1]
    lists[0:1, :pairs], right = near(left_near[...], right_near[...], per_part)
    lists[1:2, :pairs] = jnp.where(right < 2 * per_part, right ^ per_part, right)
    moves[2].wait()


def score_kernel(lists, left, pair, halo, scores, blocks, tiles, index, fetch_sem, sems):
    pairs, rows, _ = scores.shape
    vertices, width = halo.shape
    fetch = pltpu.make_async_copy(lists, index, fetch_sem)
    fetch.start()
    blocks[: 2 * vertices] = pair[...]
    blocks[2 * vertices :] = halo[...]
    fetch.wait()
    batch = pairs // sems.shape[0]
    moves = []
    for k in range(pairs):
        product = lax.dot_general(
            left[block_rows(index[0, k], rows)],
            blocks[block_rows(index[1, k], rows)],
            (((1,), (1,)), ((), ())),
            preferred_element_type=jnp.float32,
        )
        tiles[k] = (product * width**-0.5).astype(tiles.dtype)
        if (k + 1) % batch == 0:
            part = pl.ds(k + 1 - batch, batch)
            moves.append(
                pltpu.make_async_copy(tiles.at[part], scores.at[part], sems.at[k // batch])
            )
            moves[-1].start()
    for move in moves:
        move.wait()


def in_hbm(array):
    return pltpu.with_memory_space_constraint(array, pltpu.HBM)


def zigzag(cells, up):
    count = lax.axis_size("vert")
    order = list(range(0, count, 2)) + list(range(count - 1, 0, -2))
    links = list(zip(order, order[1:] + order[:1]))
    return lax.ppermute(cells, "vert", links if up else [(j, i) for i, j in links])


def chip_pair(cells):
    count = lax.axis_size("vert")
    chips = [[i, i + 1] for i in range(0, count, 2)]
    return lax.all_gather(cells, "vert", axis_index_groups=chips, tiled=True)


def body(
    features,
    tile_src,
    tile_dst,
    tile_count,
    tile_vals,
    norm_gain,
    mix_weight,
    decay_rate,
    mlp_gain,
    up_weight,
    down_weight,
    link_weight,
    pair_left,
    pair_right,
):
    _, vertices, width = features.shape
    _, slots, rows, _ = tile_vals.shape
    pairs = pair_left.shape[1]
    per_part = vertices // rows
    snaps = lax.axis_size("snap")
    hidden = up_weight.shape[1]
    bf16 = jnp.bfloat16
    f32 = jnp.float32
    shape = jax.ShapeDtypeStruct
    own = features.reshape(vertices, width)
    halo = zigzag(own, up=False)
    joined = call(
        prepare_kernel,
        shape((vertices + list_rows, width), bf16),
        VMEM,
        [SMEM] + [HBM] * 3,
        (0, 4 * vertices * width, 0),
        [
            pltpu.VMEM((1, slots), jnp.int32),
            pltpu.VMEM((1, slots), jnp.int32),
            pltpu.VMEM((1, width), jnp.int32),
            pltpu.SemaphoreType.DMA((3,)),
        ],
    )(tile_count, in_hbm(tile_src), in_hbm(tile_dst), in_hbm(own))
    tiles = lax.ppermute(
        tile_vals.reshape(slots, rows, rows),
        "vert",
        [(i, i ^ 1) for i in range(lax.axis_size("vert"))],
    )
    pair = chip_pair(joined)
    blocks, tile_lists, base, gain, out_gain = call(
        functools.partial(blocks_kernel, per_part),
        (
            shape((3 * vertices, width), bf16),
            shape((8, width // 2), jnp.int32),
            shape((vertices, width), f32),
            shape((1, width), f32),
            shape((1, width), f32),
        ),
        (VMEM,) * 5,
        [HBM] * 2 + [VMEM] * 2,
        (2**34, 8 * vertices * width, 0),
        [pltpu.SemaphoreType.DMA((2,))],
    )(
        in_hbm(norm_gain.reshape(1, width)),
        in_hbm(mlp_gain.reshape(1, width)),
        pair,
        halo,
    )
    normed = call(
        aggregate_kernel,
        shape((vertices, width), bf16),
        VMEM,
        [VMEM] * 5,
        (2 * slots * rows * rows * width, 2 * slots * rows * rows, 0),
        [
            pltpu.VMEM((vertices, width), f32),
            pltpu.VMEM((vertices, width), f32),
            pltpu.SMEM((8, width // 2), jnp.int32),
            pltpu.SemaphoreType.DMA,
        ],
    )(tile_lists, blocks, base, gain, tiles)
    by_vertex = lax.all_to_all(
        normed.reshape(snaps, vertices // snaps, width), "snap", 0, 0, tiled=True
    )
    vertex_out = call(
        vertex_kernel,
        shape(by_vertex.shape, bf16),
        VMEM,
        [VMEM] * 6,
        (
            2 * vertices * width * (2 * width + 2 * hidden),
            4 * width * (width + hidden),
            vertices * (2 * width + hidden),
        ),
    )(
        out_gain,
        by_vertex,
        mix_weight,
        decay_rate,
        up_weight,
        down_weight,
    )
    embeddings = lax.all_to_all(vertex_out, "snap", 0, 0, tiled=True).reshape(
        vertices, width
    )
    halo_out = zigzag(embeddings, up=True)
    pair_out = chip_pair(embeddings)
    left, kept, lists = call(
        functools.partial(left_kernel, per_part),
        (
            shape((vertices, width), bf16),
            shape((vertices, width), bf16),
            shape((8, width // 2), jnp.int32),
        ),
        (VMEM, ANY, VMEM),
        [HBM] * 2 + [VMEM] * 2,
        (2 * vertices * width * width, 8 * vertices * width, 0),
        [
            pltpu.VMEM((1, pairs), jnp.int32),
            pltpu.VMEM((1, pairs), jnp.int32),
            pltpu.SemaphoreType.DMA((3,)),
        ],
    )(in_hbm(pair_left), in_hbm(pair_right), pair_out, link_weight)
    scores = call(
        score_kernel,
        shape((pairs, rows, rows), bf16),
        ANY,
        [VMEM] * 4,
        (2 * pairs * rows * rows * width, 2 * pairs * rows * rows, 0),
        [
            pltpu.VMEM((3 * vertices, width), bf16),
            pltpu.VMEM((pairs, rows, rows), bf16),
            pltpu.SMEM((8, width // 2), jnp.int32),
            pltpu.SemaphoreType.DMA,
            pltpu.SemaphoreType.DMA((8,)),
        ],
    )(lists, left, pair_out, halo_out)
    return (
        kept.reshape(1, vertices, width),
        scores.reshape(1, pairs, rows, rows),
    )


def solution(mesh):
    return jax.shard_map(
        body,
        mesh=mesh,
        in_specs=(
            P("snap", "vert", None),
            P("snap", "vert"),
            P("snap", "vert"),
            P("snap", "vert"),
            P("snap", "vert", None, None),
            P(),
            P(),
            P(),
            P(),
            P(),
            P(),
            P(),
            P("snap", "vert"),
            P("snap", "vert"),
        ),
        out_specs=(P("snap", "vert", None), P("snap", "vert", None, None)),
        check_vma=False,
    )
```

```python
import functools

import jax
import jax.numpy as jnp
from jax import lax
from jax.experimental import pallas as pl
from jax.experimental.pallas import tpu as pltpu
from jax.sharding import PartitionSpec as P

epsilon = 1e-06
list_rows = 16
VMEM = pl.BlockSpec(memory_space=pltpu.VMEM)
SMEM = pl.BlockSpec(memory_space=pltpu.SMEM)


ANY = pl.BlockSpec(memory_space=pl.ANY)
HBM = pl.BlockSpec(memory_space=pltpu.HBM)


def call(kernel, outs, out_specs, in_specs, cost, scratch=()):
    flops, bytes_accessed, transcendentals = cost
    return pl.pallas_call(
        kernel,
        out_shape=outs,
        in_specs=in_specs,
        out_specs=out_specs,
        scratch_shapes=list(scratch),
        compiler_params=pltpu.CompilerParams(vmem_limit_bytes=40 * 2**20),
        cost_estimate=pl.CostEstimate(
            flops=flops, bytes_accessed=bytes_accessed, transcendentals=transcendentals
        ),
    )


def block_rows(index, rows):
    return pl.ds(pl.multiple_of(index * rows, rows), rows)


def near(own_block, other_block, per_part):
    other = other_block - (own_block & -(2 * per_part)) + 3 * per_part
    other = jnp.where(other >= 3 * per_part, other - 3 * per_part, other)
    return own_block & (per_part - 1), other


def core_index():
    return lax.rem(lax.axis_index("vert"), 2)


def prepare_kernel(
    count,
    src,
    dst,
    own,
    norm_gain,
    mlp_gain,
    joined,
    norm_gain_out,
    mlp_gain_out,
    src_near,
    dst_near,
    row,
    sems,
):
    vertices, width = own.shape
    slots = src.shape[1]
    lanes = width // 2
    moves = [
        pltpu.make_async_copy(source, target, sems.at[i])
        for i, (source, target) in enumerate(
            (
                (src, src_near),
                (dst, dst_near),
                (own, joined.at[:vertices]),
                (norm_gain, norm_gain_out),
                (mlp_gain, mlp_gain_out),
            )
        )
    ]
    for move in moves:
        move.start()
    for move in moves[:2]:
        move.wait()
    row[...] = jnp.full(row.shape, count[0, 0], jnp.int32)
    row[:, :slots] = src_near[...]
    row[:, lanes : lanes + slots] = dst_near[...]
    trailer = row[...].astype(jnp.float32).astype(joined.dtype)
    joined[vertices:] = jnp.broadcast_to(trailer, (list_rows, width))
    for move in moves[2:]:
        move.wait()


def blocks_kernel(per_part, pair, halo, blocks, index, own, lists, sem):
    vertices, width = halo.shape
    stride = pair.shape[0] // 2
    mate = 1 - core_index()
    place = pl.multiple_of(mate * stride, list_rows)
    start = pl.multiple_of(mate * stride + vertices, list_rows)
    trailer = pair[pl.ds(start, list_rows)].astype(jnp.float32)[:1].astype(jnp.int32)
    lanes = width // 2
    lists[0:1], lists[1:2] = near(trailer[:, lanes:], trailer[:, :lanes], per_part)
    lists[2:3] = trailer[:, :lanes]
    move = pltpu.make_async_copy(lists, index, sem)
    move.start()
    blocks[:vertices] = pair[:vertices]
    blocks[vertices : 2 * vertices] = pair[stride : stride + vertices]
    blocks[2 * vertices :] = halo[...]
    own[...] = pair[pl.ds(place, vertices)].astype(jnp.float32)
    move.wait()


def aggregate_kernel(index, blocks, own, gain, tiles, normed, even, odd):
    slots, rows, _ = tiles.shape
    even[...] = own[...]
    odd[...] = jnp.zeros_like(odd)
    live = index[2, slots]
    for k in range(slots):
        total = odd if k % 2 else even
        total[block_rows(index[0, k], rows)] += jnp.dot(
            jnp.where(k < live, tiles[k], jnp.zeros((), tiles.dtype)),
            blocks[block_rows(index[1, k], rows)],
            preferred_element_type=jnp.float32,
        )
    combined = even[...] + odd[...]
    scale = lax.rsqrt(jnp.mean(combined * combined, axis=-1, keepdims=True) + epsilon)
    normed[...] = (combined * scale * gain[...]).astype(normed.dtype)


def vertex_kernel(gain, normed, mix, rates, up, down, out):
    steps, rows, width = normed.shape
    projected = jnp.dot(
        normed[...].reshape(steps * rows, width),
        mix[...],
        preferred_element_type=jnp.float32,
    )
    gate = 1.0 / (1.0 + jnp.exp(-projected[:, :width]))
    state = jnp.zeros((rows, width), jnp.float32)
    states = []
    for step in range(steps):
        part = slice(step * rows, (step + 1) * rows)
        decays = jnp.exp(-rates[step : step + 1] * gate[part])
        state = decays * state + (1.0 - decays) * projected[part, width:]
        states.append(state)
    states = jnp.concatenate(states)
    scale = lax.rsqrt(jnp.mean(states * states, axis=-1, keepdims=True) + epsilon)
    state_normed = (states * scale * gain[...]).astype(jnp.bfloat16)
    inner = jnp.dot(state_normed, up[...], preferred_element_type=jnp.float32)
    hidden = (inner / (1.0 + jnp.exp(-inner))).astype(jnp.bfloat16)
    result = states + jnp.dot(hidden, down[...], preferred_element_type=jnp.float32)
    out[...] = result.astype(out.dtype).reshape(steps, rows, width)


def left_kernel(
    per_part,
    pair_left,
    pair_right,
    pair,
    link,
    left,
    kept,
    index,
    left_near,
    right_near,
    lists,
    sems,
):
    own = block_rows(1 - core_index(), left.shape[0])
    moves = [
        pltpu.make_async_copy(source, target, sems.at[i])
        for i, (source, target) in enumerate(
            ((pair_left, left_near), (pair_right, right_near), (pair.at[own], kept))
        )
    ]
    for move in moves:
        move.start()
    left[...] = jnp.dot(
        pair[own], link[...], preferred_element_type=jnp.float32
    ).astype(left.dtype)
    for move in moves[:2]:
        move.wait()
    pairs = left_near.shape[1]
    lists[0:1, :pairs], right = near(left_near[...], right_near[...], per_part)
    lists[1:2, :pairs] = jnp.where(right < 2 * per_part, right ^ per_part, right)
    fetch = pltpu.make_async_copy(lists, index, sems.at[3])
    fetch.start()
    moves[2].wait()
    fetch.wait()


def score_kernel(index, left, pair, halo, scores, blocks, tiles, sems):
    pairs, rows, _ = scores.shape
    vertices, width = halo.shape
    blocks[: 2 * vertices] = pair[...]
    blocks[2 * vertices :] = halo[...]
    batch = pairs // sems.shape[0]
    moves = []
    for k in range(pairs):
        product = lax.dot_general(
            left[block_rows(index[0, k], rows)],
            blocks[block_rows(index[1, k], rows)],
            (((1,), (1,)), ((), ())),
            preferred_element_type=jnp.float32,
        )
        tiles[k] = (product * width**-0.5).astype(tiles.dtype)
        if (k + 1) % batch == 0:
            part = pl.ds(k + 1 - batch, batch)
            moves.append(
                pltpu.make_async_copy(tiles.at[part], scores.at[part], sems.at[k // batch])
            )
            moves[-1].start()
    for move in moves:
        move.wait()


def in_hbm(array):
    return pltpu.with_memory_space_constraint(array, pltpu.HBM)


def in_smem(array):
    return pltpu.with_memory_space_constraint(array, pltpu.SMEM)


def zigzag(cells, up):
    count = lax.axis_size("vert")
    order = list(range(0, count, 2)) + list(range(count - 1, 0, -2))
    links = list(zip(order, order[1:] + order[:1]))
    return lax.ppermute(cells, "vert", links if up else [(j, i) for i, j in links])


def chip_pair(cells):
    count = lax.axis_size("vert")
    chips = [[i, i + 1] for i in range(0, count, 2)]
    return lax.all_gather(cells, "vert", axis_index_groups=chips, tiled=True)


def body(
    features,
    tile_src,
    tile_dst,
    tile_count,
    tile_vals,
    norm_gain,
    mix_weight,
    decay_rate,
    mlp_gain,
    up_weight,
    down_weight,
    link_weight,
    pair_left,
    pair_right,
):
    _, vertices, width = features.shape
    _, slots, rows, _ = tile_vals.shape
    pairs = pair_left.shape[1]
    per_part = vertices // rows
    snaps = lax.axis_size("snap")
    hidden = up_weight.shape[1]
    bf16 = jnp.bfloat16
    f32 = jnp.float32
    shape = jax.ShapeDtypeStruct
    own = features.reshape(vertices, width)
    halo = zigzag(own, up=False)
    joined, gain, out_gain = call(
        prepare_kernel,
        (
            shape((vertices + list_rows, width), bf16),
            shape((1, width), f32),
            shape((1, width), f32),
        ),
        (VMEM, VMEM, VMEM),
        [SMEM] + [HBM] * 5,
        (0, 4 * vertices * width, 0),
        [
            pltpu.VMEM((1, slots), jnp.int32),
            pltpu.VMEM((1, slots), jnp.int32),
            pltpu.VMEM((1, width), jnp.int32),
            pltpu.SemaphoreType.DMA((5,)),
        ],
    )(
        tile_count,
        in_hbm(tile_src),
        in_hbm(tile_dst),
        in_hbm(own),
        in_hbm(norm_gain.reshape(1, width)),
        in_hbm(mlp_gain.reshape(1, width)),
    )
    tiles = lax.ppermute(
        tile_vals.reshape(slots, rows, rows),
        "vert",
        [(i, i ^ 1) for i in range(lax.axis_size("vert"))],
    )
    pair = chip_pair(joined)
    blocks, tile_lists, base = call(
        functools.partial(blocks_kernel, per_part),
        (
            shape((3 * vertices, width), bf16),
            pltpu.SMEM((8, width // 2), jnp.int32),
            shape((vertices, width), f32),
        ),
        (VMEM, SMEM, VMEM),
        [VMEM] * 2,
        (2**34, 8 * vertices * width, 0),
        [pltpu.VMEM((8, width // 2), jnp.int32), pltpu.SemaphoreType.DMA],
    )(pair, halo)
    normed = call(
        aggregate_kernel,
        shape((vertices, width), bf16),
        VMEM,
        [SMEM] + [VMEM] * 4,
        (2 * slots * rows * rows * width, 2 * slots * rows * rows, 0),
        [
            pltpu.VMEM((vertices, width), f32),
            pltpu.VMEM((vertices, width), f32),
        ],
    )(in_smem(tile_lists), blocks, base, gain, tiles)
    by_vertex = lax.all_to_all(
        normed.reshape(snaps, vertices // snaps, width), "snap", 0, 0, tiled=True
    )
    vertex_out = call(
        vertex_kernel,
        shape(by_vertex.shape, bf16),
        VMEM,
        [VMEM] * 6,
        (
            2 * vertices * width * (2 * width + 2 * hidden),
            4 * width * (width + hidden),
            vertices * (2 * width + hidden),
        ),
    )(
        out_gain,
        by_vertex,
        mix_weight,
        decay_rate,
        up_weight,
        down_weight,
    )
    embeddings = lax.all_to_all(vertex_out, "snap", 0, 0, tiled=True).reshape(
        vertices, width
    )
    halo_out = zigzag(embeddings, up=True)
    pair_out = chip_pair(embeddings)
    left, kept, lists = call(
        functools.partial(left_kernel, per_part),
        (
            shape((vertices, width), bf16),
            shape((vertices, width), bf16),
            pltpu.SMEM((8, width // 2), jnp.int32),
        ),
        (VMEM, ANY, SMEM),
        [HBM] * 2 + [VMEM] * 2,
        (2 * vertices * width * width, 8 * vertices * width, 0),
        [
            pltpu.VMEM((1, pairs), jnp.int32),
            pltpu.VMEM((1, pairs), jnp.int32),
            pltpu.VMEM((8, width // 2), jnp.int32),
            pltpu.SemaphoreType.DMA((4,)),
        ],
    )(in_hbm(pair_left), in_hbm(pair_right), pair_out, link_weight)
    scores = call(
        score_kernel,
        shape((pairs, rows, rows), bf16),
        ANY,
        [SMEM] + [VMEM] * 3,
        (2 * pairs * rows * rows * width, 2 * pairs * rows * rows, 0),
        [
            pltpu.VMEM((3 * vertices, width), bf16),
            pltpu.VMEM((pairs, rows, rows), bf16),
            pltpu.SemaphoreType.DMA((8,)),
        ],
    )(in_smem(lists), left, pair_out, halo_out)
    return (
        kept.reshape(1, vertices, width),
        scores.reshape(1, pairs, rows, rows),
    )


def solution(mesh):
    return jax.shard_map(
        body,
        mesh=mesh,
        in_specs=(
            P("snap", "vert", None),
            P("snap", "vert"),
            P("snap", "vert"),
            P("snap", "vert"),
            P("snap", "vert", None, None),
            P(),
            P(),
            P(),
            P(),
            P(),
            P(),
            P(),
            P("snap", "vert"),
            P("snap", "vert"),
        ),
        out_specs=(P("snap", "vert", None), P("snap", "vert", None, None)),
        check_vma=False,
    )
```

```python
import functools

import jax
import jax.numpy as jnp
from jax import lax
from jax.experimental import pallas as pl
from jax.experimental.pallas import tpu as pltpu
from jax.sharding import PartitionSpec as P

epsilon = 1e-06
list_rows = 16
VMEM = pl.BlockSpec(memory_space=pltpu.VMEM)
SMEM = pl.BlockSpec(memory_space=pltpu.SMEM)


ANY = pl.BlockSpec(memory_space=pl.ANY)
HBM = pl.BlockSpec(memory_space=pltpu.HBM)


def call(kernel, outs, out_specs, in_specs, cost, scratch=(), aliases=None):
    flops, bytes_accessed, transcendentals = cost
    return pl.pallas_call(
        kernel,
        out_shape=outs,
        in_specs=in_specs,
        out_specs=out_specs,
        scratch_shapes=list(scratch),
        input_output_aliases=aliases or {},
        compiler_params=pltpu.CompilerParams(vmem_limit_bytes=40 * 2**20),
        cost_estimate=pl.CostEstimate(
            flops=flops, bytes_accessed=bytes_accessed, transcendentals=transcendentals
        ),
    )


def block_rows(index, rows):
    return pl.ds(pl.multiple_of(index * rows, rows), rows)


def near(own_block, other_block, per_part):
    other = other_block - (own_block & -(2 * per_part)) + 3 * per_part
    other = jnp.where(other >= 3 * per_part, other - 3 * per_part, other)
    return own_block & (per_part - 1), other


def core_index():
    return lax.rem(lax.axis_index("vert"), 2)


def prepare_kernel(
    count,
    src,
    dst,
    own,
    norm_gain,
    mlp_gain,
    joined,
    norm_gain_out,
    mlp_gain_out,
    src_near,
    dst_near,
    row,
    sems,
):
    vertices, width = own.shape
    slots = src.shape[1]
    lanes = width // 2
    moves = [
        pltpu.make_async_copy(source, target, sems.at[i])
        for i, (source, target) in enumerate(
            (
                (src, src_near),
                (dst, dst_near),
                (own, joined.at[:vertices]),
                (norm_gain, norm_gain_out),
                (mlp_gain, mlp_gain_out),
            )
        )
    ]
    for move in moves:
        move.start()
    for move in moves[:2]:
        move.wait()
    row[...] = jnp.full(row.shape, count[0, 0], jnp.int32)
    row[:, :slots] = src_near[...]
    row[:, lanes : lanes + slots] = dst_near[...]
    trailer = row[...].astype(jnp.float32).astype(joined.dtype)
    joined[vertices:] = jnp.broadcast_to(trailer, (list_rows, width))
    for move in moves[2:]:
        move.wait()


def blocks_kernel(per_part, pair, halo, blocks, index, lists, sem):
    vertices, width = halo.shape
    stride = pair.shape[0] // 2
    mate = 1 - core_index()
    start = pl.multiple_of(mate * stride + vertices, list_rows)
    trailer = pair[pl.ds(start, list_rows)].astype(jnp.float32)[:1].astype(jnp.int32)
    lanes = width // 2
    lists[0:1], lists[1:2] = near(trailer[:, lanes:], trailer[:, :lanes], per_part)
    lists[2:3] = trailer[:, :lanes]
    move = pltpu.make_async_copy(lists, index, sem)
    move.start()
    blocks[:vertices] = pair[:vertices]
    blocks[vertices : 2 * vertices] = pair[stride : stride + vertices]
    blocks[2 * vertices :] = halo[...]
    move.wait()


def aggregate_kernel(index, blocks, gain, tiles, normed, even, odd):
    slots, rows, _ = tiles.shape
    own = block_rows(1 - core_index(), even.shape[0])
    even[...] = blocks[own].astype(jnp.float32)
    odd[...] = jnp.zeros_like(odd)
    live = index[2, slots]
    for k in range(slots):
        total = odd if k % 2 else even
        total[block_rows(index[0, k], rows)] += jnp.dot(
            jnp.where(k < live, tiles[k], jnp.zeros((), tiles.dtype)),
            blocks[block_rows(index[1, k], rows)],
            preferred_element_type=jnp.float32,
        )
    combined = even[...] + odd[...]
    scale = lax.rsqrt(jnp.mean(combined * combined, axis=-1, keepdims=True) + epsilon)
    normed[...] = (combined * scale * gain[...]).astype(normed.dtype)


def vertex_kernel(gain, normed, mix, rates, up, down, out):
    steps, rows, width = normed.shape
    projected = jnp.dot(
        normed[...].reshape(steps * rows, width),
        mix[...],
        preferred_element_type=jnp.float32,
    )
    gate = 1.0 / (1.0 + jnp.exp(-projected[:, :width]))
    state = jnp.zeros((rows, width), jnp.float32)
    states = []
    for step in range(steps):
        part = slice(step * rows, (step + 1) * rows)
        decays = jnp.exp(-rates[step : step + 1] * gate[part])
        state = decays * state + (1.0 - decays) * projected[part, width:]
        states.append(state)
    states = jnp.concatenate(states)
    scale = lax.rsqrt(jnp.mean(states * states, axis=-1, keepdims=True) + epsilon)
    state_normed = (states * scale * gain[...]).astype(jnp.bfloat16)
    inner = jnp.dot(state_normed, up[...], preferred_element_type=jnp.float32)
    hidden = (inner / (1.0 + jnp.exp(-inner))).astype(jnp.bfloat16)
    result = states + jnp.dot(hidden, down[...], preferred_element_type=jnp.float32)
    out[...] = result.astype(out.dtype).reshape(steps, rows, width)


def left_kernel(
    per_part,
    pair_left,
    pair_right,
    pair,
    link,
    left,
    kept,
    index,
    blocks,
    left_near,
    right_near,
    lists,
    sems,
):
    own = block_rows(1 - core_index(), left.shape[0])
    moves = [
        pltpu.make_async_copy(source, target, sems.at[i])
        for i, (source, target) in enumerate(
            ((pair_left, left_near), (pair_right, right_near), (pair.at[own], kept))
        )
    ]
    for move in moves:
        move.start()
    left[...] = jnp.dot(
        pair[own], link[...], preferred_element_type=jnp.float32
    ).astype(left.dtype)
    for move in moves[:2]:
        move.wait()
    pairs = left_near.shape[1]
    lists[0:1, :pairs], right = near(left_near[...], right_near[...], per_part)
    lists[1:2, :pairs] = jnp.where(right < 2 * per_part, right ^ per_part, right)
    fetch = pltpu.make_async_copy(lists, index, sems.at[3])
    fetch.start()
    blocks[: pair.shape[0]] = pair[...]
    moves[2].wait()
    fetch.wait()


def score_kernel(index, left, halo, table, scores, blocks, tiles, sems):
    pairs, rows, _ = scores.shape
    vertices, width = halo.shape
    del table
    blocks[2 * vertices :] = halo[...]
    batch = pairs // sems.shape[0]
    moves = []
    for k in range(pairs):
        product = lax.dot_general(
            left[block_rows(index[0, k], rows)],
            blocks[block_rows(index[1, k], rows)],
            (((1,), (1,)), ((), ())),
            preferred_element_type=jnp.float32,
        )
        tiles[k] = (product * width**-0.5).astype(tiles.dtype)
        if (k + 1) % batch == 0:
            part = pl.ds(k + 1 - batch, batch)
            moves.append(
                pltpu.make_async_copy(tiles.at[part], scores.at[part], sems.at[k // batch])
            )
            moves[-1].start()
    for move in moves:
        move.wait()


def in_hbm(array):
    return pltpu.with_memory_space_constraint(array, pltpu.HBM)


def in_smem(array):
    return pltpu.with_memory_space_constraint(array, pltpu.SMEM)


def zigzag(cells, up):
    count = lax.axis_size("vert")
    order = list(range(0, count, 2)) + list(range(count - 1, 0, -2))
    links = list(zip(order, order[1:] + order[:1]))
    return lax.ppermute(cells, "vert", links if up else [(j, i) for i, j in links])


def chip_pair(cells):
    count = lax.axis_size("vert")
    chips = [[i, i + 1] for i in range(0, count, 2)]
    return lax.all_gather(cells, "vert", axis_index_groups=chips, tiled=True)


def body(
    features,
    tile_src,
    tile_dst,
    tile_count,
    tile_vals,
    norm_gain,
    mix_weight,
    decay_rate,
    mlp_gain,
    up_weight,
    down_weight,
    link_weight,
    pair_left,
    pair_right,
):
    _, vertices, width = features.shape
    _, slots, rows, _ = tile_vals.shape
    pairs = pair_left.shape[1]
    per_part = vertices // rows
    snaps = lax.axis_size("snap")
    hidden = up_weight.shape[1]
    bf16 = jnp.bfloat16
    f32 = jnp.float32
    shape = jax.ShapeDtypeStruct
    own = features.reshape(vertices, width)
    halo = zigzag(own, up=False)
    joined, gain, out_gain = call(
        prepare_kernel,
        (
            shape((vertices + list_rows, width), bf16),
            shape((1, width), f32),
            shape((1, width), f32),
        ),
        (VMEM, VMEM, VMEM),
        [SMEM] + [HBM] * 5,
        (0, 4 * vertices * width, 0),
        [
            pltpu.VMEM((1, slots), jnp.int32),
            pltpu.VMEM((1, slots), jnp.int32),
            pltpu.VMEM((1, width), jnp.int32),
            pltpu.SemaphoreType.DMA((5,)),
        ],
    )(
        tile_count,
        in_hbm(tile_src),
        in_hbm(tile_dst),
        in_hbm(own),
        in_hbm(norm_gain.reshape(1, width)),
        in_hbm(mlp_gain.reshape(1, width)),
    )
    tiles = lax.ppermute(
        tile_vals.reshape(slots, rows, rows),
        "vert",
        [(i, i ^ 1) for i in range(lax.axis_size("vert"))],
    )
    pair = chip_pair(joined)
    blocks, tile_lists = call(
        functools.partial(blocks_kernel, per_part),
        (
            shape((3 * vertices, width), bf16),
            pltpu.SMEM((8, width // 2), jnp.int32),
        ),
        (VMEM, SMEM),
        [VMEM] * 2,
        (2**34, 8 * vertices * width, 0),
        [pltpu.VMEM((8, width // 2), jnp.int32), pltpu.SemaphoreType.DMA],
    )(pair, halo)
    normed = call(
        aggregate_kernel,
        shape((vertices, width), bf16),
        VMEM,
        [SMEM] + [VMEM] * 3,
        (2 * slots * rows * rows * width, 2 * slots * rows * rows, 0),
        [
            pltpu.VMEM((vertices, width), f32),
            pltpu.VMEM((vertices, width), f32),
        ],
    )(in_smem(tile_lists), blocks, gain, tiles)
    by_vertex = lax.all_to_all(
        normed.reshape(snaps, vertices // snaps, width), "snap", 0, 0, tiled=True
    )
    vertex_out = call(
        vertex_kernel,
        shape(by_vertex.shape, bf16),
        VMEM,
        [VMEM] * 6,
        (
            2 * vertices * width * (2 * width + 2 * hidden),
            4 * width * (width + hidden),
            vertices * (2 * width + hidden),
        ),
    )(
        out_gain,
        by_vertex,
        mix_weight,
        decay_rate,
        up_weight,
        down_weight,
    )
    embeddings = lax.all_to_all(vertex_out, "snap", 0, 0, tiled=True).reshape(
        vertices, width
    )
    halo_out = zigzag(embeddings, up=True)
    pair_out = chip_pair(embeddings)
    left, kept, lists, table = call(
        functools.partial(left_kernel, per_part),
        (
            shape((vertices, width), bf16),
            shape((vertices, width), bf16),
            pltpu.SMEM((8, width // 2), jnp.int32),
            shape((3 * vertices, width), bf16),
        ),
        (VMEM, ANY, SMEM, VMEM),
        [HBM] * 2 + [VMEM] * 2,
        (2 * vertices * width * width, 8 * vertices * width, 0),
        [
            pltpu.VMEM((1, pairs), jnp.int32),
            pltpu.VMEM((1, pairs), jnp.int32),
            pltpu.VMEM((8, width // 2), jnp.int32),
            pltpu.SemaphoreType.DMA((4,)),
        ],
    )(in_hbm(pair_left), in_hbm(pair_right), pair_out, link_weight)
    scores, _ = call(
        score_kernel,
        (shape((pairs, rows, rows), bf16), shape(table.shape, bf16)),
        (ANY, VMEM),
        [SMEM] + [VMEM] * 3,
        (2 * pairs * rows * rows * width, 2 * pairs * rows * rows, 0),
        [pltpu.VMEM((pairs, rows, rows), bf16), pltpu.SemaphoreType.DMA((8,))],
        {3: 1},
    )(in_smem(lists), left, halo_out, table)
    return (
        kept.reshape(1, vertices, width),
        scores.reshape(1, pairs, rows, rows),
    )


def solution(mesh):
    return jax.shard_map(
        body,
        mesh=mesh,
        in_specs=(
            P("snap", "vert", None),
            P("snap", "vert"),
            P("snap", "vert"),
            P("snap", "vert"),
            P("snap", "vert", None, None),
            P(),
            P(),
            P(),
            P(),
            P(),
            P(),
            P(),
            P("snap", "vert"),
            P("snap", "vert"),
        ),
        out_specs=(P("snap", "vert", None), P("snap", "vert", None, None)),
        check_vma=False,
    )
```

```python
import functools

import jax
import jax.numpy as jnp
from jax import lax
from jax.experimental import pallas as pl
from jax.experimental.pallas import tpu as pltpu
from jax.sharding import PartitionSpec as P

epsilon = 1e-06
list_rows = 16
VMEM = pl.BlockSpec(memory_space=pltpu.VMEM)
SMEM = pl.BlockSpec(memory_space=pltpu.SMEM)


ANY = pl.BlockSpec(memory_space=pl.ANY)
HBM = pl.BlockSpec(memory_space=pltpu.HBM)


def call(kernel, outs, out_specs, in_specs, cost, scratch=()):
    flops, bytes_accessed, transcendentals = cost
    return pl.pallas_call(
        kernel,
        out_shape=outs,
        in_specs=in_specs,
        out_specs=out_specs,
        scratch_shapes=list(scratch),
        compiler_params=pltpu.CompilerParams(vmem_limit_bytes=40 * 2**20),
        cost_estimate=pl.CostEstimate(
            flops=flops, bytes_accessed=bytes_accessed, transcendentals=transcendentals
        ),
    )


def block_rows(index, rows):
    return pl.ds(pl.multiple_of(index * rows, rows), rows)


def near(own_block, other_block, per_part):
    other = other_block - (own_block & -(2 * per_part)) + 3 * per_part
    other = jnp.where(other >= 3 * per_part, other - 3 * per_part, other)
    return own_block & (per_part - 1), other


def core_index():
    return lax.rem(lax.axis_index("vert"), 2)


def prepare_kernel(
    count,
    src,
    dst,
    own,
    norm_gain,
    mlp_gain,
    joined,
    norm_gain_out,
    mlp_gain_out,
    src_near,
    dst_near,
    row,
    sems,
):
    vertices, width = own.shape
    slots = src.shape[1]
    lanes = width // 2
    moves = [
        pltpu.make_async_copy(source, target, sems.at[i])
        for i, (source, target) in enumerate(
            (
                (src, src_near),
                (dst, dst_near),
                (own, joined.at[:vertices]),
                (norm_gain, norm_gain_out),
                (mlp_gain, mlp_gain_out),
            )
        )
    ]
    for move in moves:
        move.start()
    for move in moves[:2]:
        move.wait()
    row[...] = jnp.full(row.shape, count[0, 0], jnp.int32)
    row[:, :slots] = src_near[...]
    row[:, lanes : lanes + slots] = dst_near[...]
    trailer = row[...].astype(jnp.float32).astype(joined.dtype)
    joined[vertices:] = jnp.broadcast_to(trailer, (list_rows, width))
    for move in moves[2:]:
        move.wait()


def blocks_kernel(per_part, pair, halo, blocks, index, lists, sem):
    vertices, width = halo.shape
    stride = pair.shape[0] // 2
    mate = 1 - core_index()
    start = pl.multiple_of(mate * stride + vertices, list_rows)
    trailer = pair[pl.ds(start, list_rows)].astype(jnp.float32)[:1].astype(jnp.int32)
    lanes = width // 2
    lists[0:1], lists[1:2] = near(trailer[:, lanes:], trailer[:, :lanes], per_part)
    lists[2:3] = trailer[:, :lanes]
    move = pltpu.make_async_copy(lists, index, sem)
    move.start()
    blocks[:vertices] = pair[:vertices]
    blocks[vertices : 2 * vertices] = pair[stride : stride + vertices]
    blocks[2 * vertices :] = halo[...]
    move.wait()


def aggregate_kernel(index, blocks, gain, tiles, normed, even, odd):
    slots, rows, _ = tiles.shape
    own = block_rows(1 - core_index(), even.shape[0])
    even[...] = blocks[own].astype(jnp.float32)
    odd[...] = jnp.zeros_like(odd)
    live = index[2, slots]
    for k in range(slots):
        total = odd if k % 2 else even
        total[block_rows(index[0, k], rows)] += jnp.dot(
            jnp.where(k < live, tiles[k], jnp.zeros((), tiles.dtype)),
            blocks[block_rows(index[1, k], rows)],
            preferred_element_type=jnp.float32,
        )
    combined = even[...] + odd[...]
    scale = lax.rsqrt(jnp.mean(combined * combined, axis=-1, keepdims=True) + epsilon)
    normed[...] = (combined * scale * gain[...]).astype(normed.dtype)


def vertex_kernel(gain, normed, mix, rates, up, down, out):
    steps, rows, width = normed.shape
    projected = jnp.dot(
        normed[...].reshape(steps * rows, width),
        mix[...],
        preferred_element_type=jnp.float32,
    )
    gate = 0.5 + 0.5 * jnp.tanh(0.5 * projected[:, :width])
    state = jnp.zeros((rows, width), jnp.float32)
    states = []
    for step in range(steps):
        part = slice(step * rows, (step + 1) * rows)
        decays = jnp.exp(-rates[step : step + 1] * gate[part])
        state = decays * state + (1.0 - decays) * projected[part, width:]
        states.append(state)
    states = jnp.concatenate(states)
    scale = lax.rsqrt(jnp.mean(states * states, axis=-1, keepdims=True) + epsilon)
    state_normed = (states * scale * gain[...]).astype(jnp.bfloat16)
    inner = jnp.dot(state_normed, up[...], preferred_element_type=jnp.float32)
    half = 0.5 * inner
    hidden = (half + half * jnp.tanh(half)).astype(jnp.bfloat16)
    result = states + jnp.dot(hidden, down[...], preferred_element_type=jnp.float32)
    out[...] = result.astype(out.dtype).reshape(steps, rows, width)


def left_kernel(
    per_part,
    pair_left,
    pair_right,
    pair,
    link,
    left,
    kept,
    index,
    left_near,
    right_near,
    lists,
    sems,
):
    own = block_rows(1 - core_index(), left.shape[0])
    moves = [
        pltpu.make_async_copy(source, target, sems.at[i])
        for i, (source, target) in enumerate(
            ((pair_left, left_near), (pair_right, right_near), (pair.at[own], kept))
        )
    ]
    for move in moves:
        move.start()
    left[...] = jnp.dot(
        pair[own], link[...], preferred_element_type=jnp.float32
    ).astype(left.dtype)
    for move in moves[:2]:
        move.wait()
    pairs = left_near.shape[1]
    lists[0:1, :pairs], right = near(left_near[...], right_near[...], per_part)
    lists[1:2, :pairs] = jnp.where(right < 2 * per_part, right ^ per_part, right)
    fetch = pltpu.make_async_copy(lists, index, sems.at[3])
    fetch.start()
    moves[2].wait()
    fetch.wait()


def score_kernel(index, left, pair, halo, scores, blocks, tiles, sems):
    pairs, rows, _ = scores.shape
    vertices, width = halo.shape
    blocks[: 2 * vertices] = pair[...]
    blocks[2 * vertices :] = halo[...]
    batch = pairs // sems.shape[0]
    moves = []
    for k in range(pairs):
        product = lax.dot_general(
            left[block_rows(index[0, k], rows)],
            blocks[block_rows(index[1, k], rows)],
            (((1,), (1,)), ((), ())),
            preferred_element_type=jnp.float32,
        )
        tiles[k] = (product * width**-0.5).astype(tiles.dtype)
        if (k + 1) % batch == 0:
            part = pl.ds(k + 1 - batch, batch)
            moves.append(
                pltpu.make_async_copy(tiles.at[part], scores.at[part], sems.at[k // batch])
            )
            moves[-1].start()
    for move in moves:
        move.wait()


def in_hbm(array):
    return pltpu.with_memory_space_constraint(array, pltpu.HBM)


def in_smem(array):
    return pltpu.with_memory_space_constraint(array, pltpu.SMEM)


def zigzag(cells, up):
    count = lax.axis_size("vert")
    order = list(range(0, count, 2)) + list(range(count - 1, 0, -2))
    links = list(zip(order, order[1:] + order[:1]))
    return lax.ppermute(cells, "vert", links if up else [(j, i) for i, j in links])


def chip_pair(cells):
    count = lax.axis_size("vert")
    chips = [[i, i + 1] for i in range(0, count, 2)]
    return lax.all_gather(cells, "vert", axis_index_groups=chips, tiled=True)


def body(
    features,
    tile_src,
    tile_dst,
    tile_count,
    tile_vals,
    norm_gain,
    mix_weight,
    decay_rate,
    mlp_gain,
    up_weight,
    down_weight,
    link_weight,
    pair_left,
    pair_right,
):
    _, vertices, width = features.shape
    _, slots, rows, _ = tile_vals.shape
    pairs = pair_left.shape[1]
    per_part = vertices // rows
    snaps = lax.axis_size("snap")
    hidden = up_weight.shape[1]
    bf16 = jnp.bfloat16
    f32 = jnp.float32
    shape = jax.ShapeDtypeStruct
    own = features.reshape(vertices, width)
    halo = zigzag(own, up=False)
    joined, gain, out_gain = call(
        prepare_kernel,
        (
            shape((vertices + list_rows, width), bf16),
            shape((1, width), f32),
            shape((1, width), f32),
        ),
        (VMEM, VMEM, VMEM),
        [SMEM] + [HBM] * 5,
        (0, 4 * vertices * width, 0),
        [
            pltpu.VMEM((1, slots), jnp.int32),
            pltpu.VMEM((1, slots), jnp.int32),
            pltpu.VMEM((1, width), jnp.int32),
            pltpu.SemaphoreType.DMA((5,)),
        ],
    )(
        tile_count,
        in_hbm(tile_src),
        in_hbm(tile_dst),
        in_hbm(own),
        in_hbm(norm_gain.reshape(1, width)),
        in_hbm(mlp_gain.reshape(1, width)),
    )
    tiles = lax.ppermute(
        tile_vals.reshape(slots, rows, rows),
        "vert",
        [(i, i ^ 1) for i in range(lax.axis_size("vert"))],
    )
    pair = chip_pair(joined)
    blocks, tile_lists = call(
        functools.partial(blocks_kernel, per_part),
        (
            shape((3 * vertices, width), bf16),
            pltpu.SMEM((8, width // 2), jnp.int32),
        ),
        (VMEM, SMEM),
        [VMEM] * 2,
        (2**34, 8 * vertices * width, 0),
        [pltpu.VMEM((8, width // 2), jnp.int32), pltpu.SemaphoreType.DMA],
    )(pair, halo)
    normed = call(
        aggregate_kernel,
        shape((vertices, width), bf16),
        VMEM,
        [SMEM] + [VMEM] * 3,
        (2 * slots * rows * rows * width, 2 * slots * rows * rows, 0),
        [
            pltpu.VMEM((vertices, width), f32),
            pltpu.VMEM((vertices, width), f32),
        ],
    )(in_smem(tile_lists), blocks, gain, tiles)
    by_vertex = lax.all_to_all(
        normed.reshape(snaps, vertices // snaps, width), "snap", 0, 0, tiled=True
    )
    vertex_out = call(
        vertex_kernel,
        shape(by_vertex.shape, bf16),
        VMEM,
        [VMEM] * 6,
        (
            2 * vertices * width * (2 * width + 2 * hidden),
            4 * width * (width + hidden),
            vertices * (2 * width + hidden),
        ),
    )(
        out_gain,
        by_vertex,
        mix_weight,
        decay_rate,
        up_weight,
        down_weight,
    )
    embeddings = lax.all_to_all(vertex_out, "snap", 0, 0, tiled=True).reshape(
        vertices, width
    )
    halo_out = zigzag(embeddings, up=True)
    pair_out = chip_pair(embeddings)
    left, kept, lists = call(
        functools.partial(left_kernel, per_part),
        (
            shape((vertices, width), bf16),
            shape((vertices, width), bf16),
            pltpu.SMEM((8, width // 2), jnp.int32),
        ),
        (VMEM, ANY, SMEM),
        [HBM] * 2 + [VMEM] * 2,
        (2 * vertices * width * width, 8 * vertices * width, 0),
        [
            pltpu.VMEM((1, pairs), jnp.int32),
            pltpu.VMEM((1, pairs), jnp.int32),
            pltpu.VMEM((8, width // 2), jnp.int32),
            pltpu.SemaphoreType.DMA((4,)),
        ],
    )(in_hbm(pair_left), in_hbm(pair_right), pair_out, link_weight)
    scores = call(
        score_kernel,
        shape((pairs, rows, rows), bf16),
        ANY,
        [SMEM] + [VMEM] * 3,
        (2 * pairs * rows * rows * width, 2 * pairs * rows * rows, 0),
        [
            pltpu.VMEM((3 * vertices, width), bf16),
            pltpu.VMEM((pairs, rows, rows), bf16),
            pltpu.SemaphoreType.DMA((8,)),
        ],
    )(in_smem(lists), left, pair_out, halo_out)
    return (
        kept.reshape(1, vertices, width),
        scores.reshape(1, pairs, rows, rows),
    )


def solution(mesh):
    return jax.shard_map(
        body,
        mesh=mesh,
        in_specs=(
            P("snap", "vert", None),
            P("snap", "vert"),
            P("snap", "vert"),
            P("snap", "vert"),
            P("snap", "vert", None, None),
            P(),
            P(),
            P(),
            P(),
            P(),
            P(),
            P(),
            P("snap", "vert"),
            P("snap", "vert"),
        ),
        out_specs=(P("snap", "vert", None), P("snap", "vert", None, None)),
        check_vma=False,
    )
```
